32 devices in a mesh: seq: 8 (over z, x), chan: 4 (over y, core).
Axes of the slice: x: 2, y: 2, z: 4, core: 2. Of those that a mesh axis runs over, the one named last changes fastest.
Arguments:
- value_in: bfloat16 [3072, 4096], P('seq', 'chan'), may hold values from -6 to 6
- gate_in: bfloat16 [3072, 4096], P('seq', 'chan'), may hold values from -6 to 6
- gate_out: bfloat16 [3072, 4096], P('seq', 'chan'), may hold values from -6 to 6
- spectral_filter: bfloat16 [3072, 4096], P('seq', 'chan'), may hold values from -6 to 6
- analysis_blocks: bfloat16 [3, 128, 128], replicated, may hold values from -0.5 to 0.5
- analysis_mix: bfloat16 [128, 3, 3], replicated, may hold values from -3.5 to 3.5
- synthesis_blocks: bfloat16 [3, 128, 128], replicated, may hold values from -0.5 to 0.5
- synthesis_mix: bfloat16 [128, 3, 3], replicated, may hold values from -3.5 to 3.5
- angles: float32 [3, 384], replicated, may hold values from -3.140625 to 3.140625
- out_weight: bfloat16 [4096, 4096], P('chan'), may hold values from -0.09375 to 0.09375
Outputs:
- projected: bfloat16 [3072, 4096], P(('seq', 'chan'))
The draws below stay inside these ranges and needn't reach their ends.
All inputs are finite; a program needn't handle non-finite values.
Results may differ from the reference program's by a relative error of at most 0.02.
Values may be sent and summed in bfloat16 or wider, within the bound.
A program may use at most 64 MiB of HBM per device.

```python
import jax
import jax.numpy as jnp
from jax import lax

WIDTH = 4096
BLOCK = 128
TOK_DEV = 384
NB = 3
SECTIONS = 3
LENGTH = 3072
N_SEQ = 8


def block_levels(rng, shape, cuts, low, high):
    factor_of, own = 1.0, jax.random.fold_in(rng, 6)
    for axis_at, blocks in cuts:
        heights = jnp.exp(jax.random.uniform(jax.random.fold_in(own, axis_at), (blocks,), jnp.float32, low / len(cuts), high / len(cuts)))
        factor_of = factor_of * jnp.repeat(heights, shape[axis_at] // blocks).reshape([-1 if axis == axis_at else 1 for axis in range(len(shape))])
    return factor_of


def scatter_about(own_key, extent, scale, limit, split=(), held_as=jnp.bfloat16):
    loudness = block_levels(own_key, extent, split, -0.22, 0.18) if split else 1.0
    values = jax.random.normal(own_key, extent, jnp.float32) * scale * loudness
    return jnp.minimum(jnp.maximum(values, -limit), limit).astype(held_as)


def setup_inputs(seed: int = 0) -> dict:
    arg_keys = jax.random.split(jax.random.key(seed), 11)
    return {
        "value_in": scatter_about(arg_keys[0], (LENGTH, WIDTH), 1.0, 6.0, ((0, 8), (1, 4))),
        "gate_in": scatter_about(arg_keys[1], (LENGTH, WIDTH), 1.0, 6.0, ((0, 8), (1, 4))),
        "gate_out": scatter_about(arg_keys[2], (LENGTH, WIDTH), 1.0, 6.0, ((0, 8), (1, 4))),
        "spectral_filter": scatter_about(arg_keys[3], (LENGTH, WIDTH), 1.0, 6.0, ((0, 8), (1, 4))),
        "analysis_blocks": scatter_about(arg_keys[4], (NB, BLOCK, BLOCK), BLOCK ** -0.5, 0.5),
        "analysis_mix": scatter_about(arg_keys[5], (BLOCK, NB, NB), NB ** -0.5, 3.5),
        "synthesis_blocks": scatter_about(arg_keys[6], (NB, BLOCK, BLOCK), BLOCK ** -0.5, 0.5),
        "synthesis_mix": scatter_about(arg_keys[7], (BLOCK, NB, NB), NB ** -0.5, 3.5),
        "angles": jnp.clip(jax.random.uniform(arg_keys[8], (SECTIONS, TOK_DEV), jnp.float32, -3.140625, 3.140625), -3.140625, 3.140625),
        "out_weight": scatter_about(arg_keys[9], (WIDTH, WIDTH), WIDTH ** -0.5, 0.09375, ((0, 4),)),
    }


def rotate_section(values, theta, width, flip):
    count = values.shape[0]
    shaped = values.reshape((count // (2 * width), 2, width) + values.shape[1:]).astype(jnp.float32)
    cosine = jnp.cos(theta)[:, :, None]
    sine = flip * jnp.sin(theta)[:, :, None]
    lower = shaped[:, 0]
    upper = shaped[:, 1]
    new_lower = cosine * lower + sine * upper
    new_upper = cosine * upper - sine * lower
    return jnp.stack([new_lower, new_upper], axis=1).reshape(values.shape).astype(jnp.bfloat16)


def reference(value_in, gate_in, gate_out, spectral_filter, analysis_blocks, analysis_mix, synthesis_blocks, synthesis_mix, angles, out_weight):
    grid = (N_SEQ, NB, BLOCK, WIDTH)
    mixed = (gate_in.astype(jnp.float32) * value_in.astype(jnp.float32)).astype(jnp.bfloat16).reshape(grid)
    inner = jnp.einsum('kij,nkjc->nkic', analysis_blocks.astype(jnp.float32), mixed.astype(jnp.float32)).astype(jnp.bfloat16)
    inner = lax.optimization_barrier(inner)
    spec = jnp.einsum('ikl,nlic->nkic', analysis_mix.astype(jnp.float32), inner.astype(jnp.float32)).astype(jnp.bfloat16)
    theta = angles.reshape(SECTIONS, NB, BLOCK)
    for section in range(SECTIONS):
        spec = rotate_section(spec, theta[section], 2 ** section, 1.0)
    spec = (spec.astype(jnp.float32) * spectral_filter.reshape(grid).astype(jnp.float32)).astype(jnp.bfloat16)
    for section in reversed(range(SECTIONS)):
        spec = rotate_section(spec, theta[section], 2 ** section, -1.0)
    spread = jnp.einsum('ikl,nlic->nkic', synthesis_mix.astype(jnp.float32), spec.astype(jnp.float32)).astype(jnp.bfloat16)
    spread = lax.optimization_barrier(spread)
    conv = jnp.einsum('kij,nkjc->nkic', synthesis_blocks.astype(jnp.float32), spread.astype(jnp.float32))
    gated = (gate_out.astype(jnp.float32) * conv.reshape(N_SEQ * NB * BLOCK, WIDTH)).astype(jnp.bfloat16)
    return jnp.dot(gated, out_weight, preferred_element_type=jnp.float32).astype(jnp.bfloat16)
```

```python
import functools

import jax
import jax.numpy as jnp
from jax import lax
from jax.experimental import pallas as pl
from jax.experimental.pallas import tpu as pltpu
from jax.sharding import PartitionSpec as P

MESH = pl.DeviceIdType.MESH
LANES = 128
PIECES = 3
STEP = 16
COLS = 512
F32 = jnp.float32
BF16 = jnp.bfloat16


def kernel(
    n,
    lane_groups,
    value_ref,
    gate_ref,
    filter_ref,
    gate_out_ref,
    analysis_ref,
    synthesis_ref,
    mix_ref,
    table_ref,
    weight_ref,
    out_ref,
    xsend,
    xs,
    fs,
    ysend,
    yr,
    gate_out,
    weight,
    gated,
    part,
    first,
    second_send,
    second,
    f_send,
    f_recv,
    x_send,
    x_recv,
    y_send,
    y_recv,
    local_sem,
    first_send_sem,
    first_recv_sem,
    second_send_sem,
    second_recv_sem,
):
    me = lax.axis_index("seq")
    chan = lax.axis_index("chan")
    core = lax.rem(chan, 2)
    side = chan // 2
    core_peer = chan + 1 - 2 * core
    side_peer = (1 - side) * 2 + core
    tokens = value_ref.shape[0]
    nb, blk, _ = analysis_ref.shape
    row_groups = n // lane_groups
    rows = tokens // row_groups
    piece = rows // PIECES
    sections = n.bit_length() - 1

    barrier = pltpu.get_barrier_semaphore()
    for s in range(1, n):
        pl.semaphore_signal(barrier, inc=1, device_id={"seq": me ^ s}, device_id_type=MESH)
    pl.semaphore_signal(barrier, inc=1, device_id={"chan": core_peer}, device_id_type=MESH)
    pl.semaphore_signal(barrier, inc=1, device_id={"chan": side_peer}, device_id_type=MESH)
    pl.semaphore_wait(barrier, n + 1)

    def chunk_lanes(index):
        return pl.ds(pl.multiple_of(lax.rem(index, lane_groups) * LANES, LANES), LANES)

    def chunk_row(index):
        return pl.multiple_of((index // lane_groups) * rows, STEP)

    my_row = chunk_row(me)

    for s in range(n - 1, 0, -1):
        there = me ^ s
        pltpu.make_async_remote_copy(
            src_ref=filter_ref.at[pl.ds(chunk_row(there), rows), chunk_lanes(there)],
            dst_ref=fs.at[s],
            send_sem=f_send,
            recv_sem=f_recv,
            device_id={"seq": there},
            device_id_type=MESH,
        ).start()
    own_filter = pltpu.make_async_copy(
        filter_ref.at[pl.ds(my_row, rows), chunk_lanes(me)], fs.at[0], local_sem.at[0]
    )
    own_filter.start()
    weight_copy = pltpu.make_async_copy(weight_ref, weight, local_sem.at[1])
    weight_copy.start()
    gate_copy = pltpu.make_async_copy(gate_out_ref, gate_out, local_sem.at[2])
    gate_copy.start()

    def analyse(step, carry):
        t = lane_groups - 1 - step
        lanes = pl.ds(
            pl.multiple_of((lax.rem(me, lane_groups) ^ t) * LANES, LANES), LANES
        )
        mixed = (gate_ref[:, lanes].astype(F32) * value_ref[:, lanes].astype(F32)).astype(BF16)
        inner = [
            jnp.dot(
                analysis_ref[k], mixed[k * blk : (k + 1) * blk], preferred_element_type=F32
            )
            .astype(BF16)
            .astype(F32)
            for k in range(nb)
        ]
        for k in range(nb):
            total = mix_ref[:, k * nb : k * nb + 1] * inner[0]
            for other in range(1, nb):
                at = k * nb + other
                total += mix_ref[:, at : at + 1] * inner[other]
            xsend[t, pl.ds(k * blk, blk), :] = total.astype(BF16)
        return carry

    lax.fori_loop(0, lane_groups, analyse, 0)
    xs[0] = xsend[0, pl.ds(my_row, rows), :]
    for p in range(PIECES):
        for s in range(n - 1, 0, -1):
            there = me ^ s
            pltpu.make_async_remote_copy(
                src_ref=xsend.at[
                    s % lane_groups,
                    pl.ds(pl.multiple_of(chunk_row(there) + p * piece, STEP), piece),
                ],
                dst_ref=xs.at[s, pl.ds(p * piece, piece)],
                send_sem=x_send.at[p],
                recv_sem=x_recv.at[p],
                device_id={"seq": there},
                device_id_type=MESH,
            ).start()

    def others(ref, p):
        return ref.at[pl.ds(1, n - 1), pl.ds(p * piece, piece)]

    def wait_bytes(ref, sem):
        pltpu.make_async_copy(ref, ref, sem).wait()

    own_filter.wait()
    wait_bytes(fs.at[pl.ds(1, n - 1)], f_recv)
    for p in range(PIECES):
        wait_bytes(others(xs, p), x_recv.at[p])

        def rotate(step, carry):
            at = pl.multiple_of(p * piece + step * STEP, STEP)
            here = pl.multiple_of(my_row + at, STEP)
            spec = [xs[s, pl.ds(at, STEP), :].astype(F32) for s in range(n)]
            cosine = [table_ref[pl.ds(here, STEP), b : b + 1] for b in range(sections)]
            sine = [
                table_ref[pl.ds(here, STEP), sections + b : sections + b + 1]
                for b in range(sections)
            ]

            def section(spec, b, flip):
                plus, minus = (sine[b], -sine[b]) if flip > 0 else (-sine[b], sine[b])
                return [
                    cosine[b] * spec[s] + (minus if s >> b & 1 else plus) * spec[s ^ (1 << b)]
                    for s in range(n)
                ]

            for b in range(sections):
                spec = section(spec, b, 1)
            spec = [spec[s] * fs[s, pl.ds(at, STEP), :].astype(F32) for s in range(n)]
            for b in reversed(range(sections)):
                spec = section(spec, b, -1)
            yr[0, pl.ds(here, STEP), :] = spec[0].astype(BF16)
            for s in range(1, n):
                ysend[s, pl.ds(at, STEP), :] = spec[s].astype(BF16)
            return carry

        lax.fori_loop(0, piece // STEP, rotate, 0)
        for s in range(n - 1, 0, -1):
            pltpu.make_async_remote_copy(
                src_ref=ysend.at[s, pl.ds(p * piece, piece)],
                dst_ref=yr.at[
                    s % lane_groups, pl.ds(pl.multiple_of(my_row + p * piece, STEP), piece)
                ],
                send_sem=y_send.at[p],
                recv_sem=y_recv.at[p],
                device_id={"seq": me ^ s},
                device_id_type=MESH,
            ).start()

    gate_copy.wait()
    for p in range(PIECES):
        wait_bytes(others(ysend, p), y_recv.at[p])

    def synthesise(t, carry):
        lanes = pl.ds(
            pl.multiple_of((lax.rem(me, lane_groups) ^ t) * LANES, LANES), LANES
        )
        back = [yr[t, pl.ds(k * blk, blk), :].astype(F32) for k in range(nb)]
        for k in range(nb):
            at = nb * nb + k * nb
            total = mix_ref[:, at : at + 1] * back[0]
            for other in range(1, nb):
                total += mix_ref[:, at + other : at + other + 1] * back[other]
            conv = jnp.dot(synthesis_ref[k], total.astype(BF16), preferred_element_type=F32)
            gated[pl.ds(k * blk, blk), lanes] = (
                gate_out[pl.ds(k * blk, blk), lanes].astype(F32) * conv
            ).astype(BF16)
        return carry

    lax.fori_loop(0, lane_groups, synthesise, 0)
    weight_copy.wait()

    share = tokens // 4
    blocks = weight.shape[1] // COLS

    def columns(q):
        return pl.ds(pl.multiple_of(q * COLS, COLS), COLS)

    def to_core(q):
        return pltpu.make_async_remote_copy(
            src_ref=part.at[q, 1 - core],
            dst_ref=first.at[q],
            send_sem=first_send_sem.at[q],
            recv_sem=first_recv_sem.at[q],
            device_id={"chan": core_peer},
            device_id_type=MESH,
        )

    def to_side(q):
        return pltpu.make_async_remote_copy(
            src_ref=second_send.at[q],
            dst_ref=second.at[q],
            send_sem=second_send_sem.at[q],
            recv_sem=second_recv_sem.at[q],
            device_id={"chan": side_peer},
            device_id_type=MESH,
        )

    def forward(q):
        to_core(q).wait_recv()
        second_send[q] = (
            part[q, core, 1 - side].astype(F32) + first[q, 1 - side].astype(F32)
        ).astype(BF16)
        to_side(q).start()

    def project(q, carry):
        product = jnp.dot(gated[...], weight[:, columns(q)], preferred_element_type=F32)
        for g in range(4):
            part[q, g % 2, g // 2] = product[g * share : (g + 1) * share].astype(BF16)
        to_core(q).start()

        @pl.when(q > 0)
        def _():
            forward(q - 1)

        return carry

    lax.fori_loop(0, blocks, project, 0)
    forward(blocks - 1)

    def finish(q, carry):
        to_side(q).wait_recv()
        out_ref[:, columns(q)] = (
            part[q, core, side].astype(F32)
            + first[q, side].astype(F32)
            + second[q].astype(F32)
        ).astype(BF16)
        to_core(q).wait_send()
        to_side(q).wait_send()
        return carry

    lax.fori_loop(0, blocks, finish, 0)
    wait_bytes(fs.at[pl.ds(1, n - 1)], f_send)
    for p in range(PIECES):
        wait_bytes(others(xs, p), x_send.at[p])
        wait_bytes(others(ysend, p), y_send.at[p])


def per_device(
    value_in,
    gate_in,
    gate_out,
    spectral_filter,
    analysis_blocks,
    analysis_mix,
    synthesis_blocks,
    synthesis_mix,
    angles,
    out_weight,
):
    tokens, chans = value_in.shape
    blk = analysis_blocks.shape[1]
    width = out_weight.shape[1]
    n = lax.axis_size("seq")
    sections = n.bit_length() - 1
    lane_groups = min(n, chans // LANES)
    rows = tokens // (n // lane_groups)
    blocks = width // COLS
    share = tokens // 4
    bit = lax.axis_index("seq") >> jnp.arange(sections) & 1
    sign = (1 - 2 * bit).astype(F32)[:, None]
    table = jnp.concatenate([jnp.cos(angles), sign * jnp.sin(angles)], axis=0).T
    mix = jnp.concatenate(
        [analysis_mix.reshape(blk, -1), synthesis_mix.reshape(blk, -1)], axis=1
    ).astype(F32)
    vmem = pl.BlockSpec(memory_space=pltpu.VMEM)
    anywhere = pl.BlockSpec(memory_space=pl.ANY)
    chunk = pltpu.VMEM((n, rows, LANES), BF16)
    whole = pltpu.VMEM((lane_groups, tokens, LANES), BF16)
    return pl.pallas_call(
        functools.partial(kernel, n, lane_groups),
        out_shape=jax.ShapeDtypeStruct((share, width), BF16),
        in_specs=[vmem, vmem, anywhere, anywhere, vmem, vmem, vmem, vmem, anywhere],
        out_specs=vmem,
        scratch_shapes=[
            whole,
            chunk,
            chunk,
            chunk,
            whole,
            pltpu.VMEM((tokens, chans), BF16),
            pltpu.VMEM(out_weight.shape, BF16),
            pltpu.VMEM((tokens, chans), BF16),
            pltpu.VMEM((blocks, 2, 2, share, COLS), BF16),
            pltpu.VMEM((blocks, 2, share, COLS), BF16),
            pltpu.VMEM((blocks, share, COLS), BF16),
            pltpu.VMEM((blocks, share, COLS), BF16),
            pltpu.SemaphoreType.DMA,
            pltpu.SemaphoreType.DMA,
            pltpu.SemaphoreType.DMA((PIECES,)),
            pltpu.SemaphoreType.DMA((PIECES,)),
            pltpu.SemaphoreType.DMA((PIECES,)),
            pltpu.SemaphoreType.DMA((PIECES,)),
            pltpu.SemaphoreType.DMA((3,)),
            pltpu.SemaphoreType.DMA((blocks,)),
            pltpu.SemaphoreType.DMA((blocks,)),
            pltpu.SemaphoreType.DMA((blocks,)),
            pltpu.SemaphoreType.DMA((blocks,)),
        ],
        compiler_params=pltpu.CompilerParams(
            collective_id=0, has_side_effects=True, vmem_limit_bytes=48 * 2**20
        ),
    )(
        value_in,
        gate_in,
        spectral_filter,
        gate_out,
        analysis_blocks,
        synthesis_blocks,
        mix,
        table,
        out_weight,
    )


def solution(mesh):
    placed = (
        P("seq", "chan"),
        P("seq", "chan"),
        P("seq", "chan"),
        P("seq", "chan"),
        P(),
        P(),
        P(),
        P(),
        P(),
        P("chan", None),
    )
    return jax.shard_map(
        per_device, mesh=mesh, in_specs=placed, out_specs=P(("seq", "chan"), None), check_vma=False
    )
```

```python
import functools

import jax
import jax.numpy as jnp
from jax import lax
from jax.experimental import pallas as pl
from jax.experimental.pallas import tpu as pltpu
from jax.sharding import PartitionSpec as P

MESH = pl.DeviceIdType.MESH
LANES = 128
PIECES = 3
STEP = 16
COLS = 512
F32 = jnp.float32
BF16 = jnp.bfloat16


def kernel(
    n,
    lane_groups,
    value_hbm,
    gate_hbm,
    filter_ref,
    gate_out_ref,
    analysis_hbm,
    synthesis_hbm,
    analysis_mix_hbm,
    synthesis_mix_hbm,
    angles_hbm,
    weight_ref,
    out_ref,
    value_ref,
    gate_ref,
    analysis_ref,
    synthesis_ref,
    analysis_mix,
    synthesis_mix,
    angles,
    mix_ref,
    table_ref,
    wide,
    xsend,
    xs,
    fs,
    ysend,
    yr,
    gate_out,
    weight,
    gated,
    part,
    first,
    second_send,
    second,
    f_send,
    f_recv,
    x_send,
    x_recv,
    y_send,
    y_recv,
    local_sem,
    load_sem,
    first_send_sem,
    first_recv_sem,
    second_send_sem,
    second_recv_sem,
):
    me = lax.axis_index("seq")
    chan = lax.axis_index("chan")
    core = lax.rem(chan, 2)
    side = chan // 2
    core_peer = chan + 1 - 2 * core
    side_peer = (1 - side) * 2 + core
    tokens = value_hbm.shape[0]
    nb, blk, _ = analysis_hbm.shape
    row_groups = n // lane_groups
    rows = tokens // row_groups
    piece = rows // PIECES
    sections = n.bit_length() - 1

    loads = [
        pltpu.make_async_copy(source, target, load_sem.at[at])
        for at, (source, target) in enumerate(
            (
                (value_hbm, value_ref),
                (gate_hbm, gate_ref),
                (analysis_hbm, analysis_ref),
                (analysis_mix_hbm, analysis_mix),
                (synthesis_mix_hbm, synthesis_mix),
                (angles_hbm, angles),
                (synthesis_hbm, synthesis_ref),
            )
        )
    ]
    for load in loads:
        load.start()

    barrier = pltpu.get_barrier_semaphore()
    for s in range(1, n):
        pl.semaphore_signal(barrier, inc=1, device_id={"seq": me ^ s}, device_id_type=MESH)
    pl.semaphore_signal(barrier, inc=1, device_id={"chan": core_peer}, device_id_type=MESH)
    pl.semaphore_signal(barrier, inc=1, device_id={"chan": side_peer}, device_id_type=MESH)
    pl.semaphore_wait(barrier, n + 1)

    def chunk_lanes(index):
        return pl.ds(pl.multiple_of(lax.rem(index, lane_groups) * LANES, LANES), LANES)

    def chunk_row(index):
        return pl.multiple_of((index // lane_groups) * rows, STEP)

    my_row = chunk_row(me)

    for s in range(n - 1, 0, -1):
        there = me ^ s
        pltpu.make_async_remote_copy(
            src_ref=filter_ref.at[pl.ds(chunk_row(there), rows), chunk_lanes(there)],
            dst_ref=fs.at[s],
            send_sem=f_send,
            recv_sem=f_recv,
            device_id={"seq": there},
            device_id_type=MESH,
        ).start()
    own_filter = pltpu.make_async_copy(
        filter_ref.at[pl.ds(my_row, rows), chunk_lanes(me)], fs.at[0], local_sem.at[0]
    )
    own_filter.start()
    weight_copy = pltpu.make_async_copy(weight_ref, weight, local_sem.at[1])
    weight_copy.start()
    gate_copy = pltpu.make_async_copy(gate_out_ref, gate_out, local_sem.at[2])
    gate_copy.start()

    for load in loads:
        load.wait()

    wide[...] = jnp.zeros_like(wide)
    for which, source in enumerate((analysis_mix, synthesis_mix)):
        for k in range(nb):
            at = (which * nb + k) * nb
            wide[pl.ds(at, nb), :] = source[k].astype(F32)
    mix_ref[...] = wide[...].T

    def analyse(step, carry):
        t = lane_groups - 1 - step
        lanes = pl.ds(
            pl.multiple_of((lax.rem(me, lane_groups) ^ t) * LANES, LANES), LANES
        )
        mixed = (gate_ref[:, lanes].astype(F32) * value_ref[:, lanes].astype(F32)).astype(BF16)
        inner = [
            jnp.dot(
                analysis_ref[k], mixed[k * blk : (k + 1) * blk], preferred_element_type=F32
            )
            .astype(BF16)
            .astype(F32)
            for k in range(nb)
        ]
        for k in range(nb):
            total = mix_ref[:, k * nb : k * nb + 1] * inner[0]
            for other in range(1, nb):
                at = k * nb + other
                total += mix_ref[:, at : at + 1] * inner[other]
            xsend[t, pl.ds(k * blk, blk), :] = total.astype(BF16)
        return carry

    lax.fori_loop(0, lane_groups, analyse, 0)
    xs[0] = xsend[0, pl.ds(my_row, rows), :]
    for p in range(PIECES):
        for s in range(n - 1, 0, -1):
            there = me ^ s
            pltpu.make_async_remote_copy(
                src_ref=xsend.at[
                    s % lane_groups,
                    pl.ds(pl.multiple_of(chunk_row(there) + p * piece, STEP), piece),
                ],
                dst_ref=xs.at[s, pl.ds(p * piece, piece)],
                send_sem=x_send.at[p],
                recv_sem=x_recv.at[p],
                device_id={"seq": there},
                device_id_type=MESH,
            ).start()

    for k in range(nb):
        theta = angles[:, pl.ds(k * blk, blk)]
        cosine, sine = jnp.cos(theta), jnp.sin(theta)
        for b in range(sections):
            sign = (1 - 2 * (me >> b & 1)).astype(F32)
            wide[pl.ds(b, 1), :] = cosine[b : b + 1]
            wide[pl.ds(sections + b, 1), :] = sine[b : b + 1] * sign
        table_ref[pl.ds(k * blk, blk), :] = wide[...].T

    def others(ref, p):
        return ref.at[pl.ds(1, n - 1), pl.ds(p * piece, piece)]

    def wait_bytes(ref, sem):
        pltpu.make_async_copy(ref, ref, sem).wait()

    own_filter.wait()
    wait_bytes(fs.at[pl.ds(1, n - 1)], f_recv)
    for p in range(PIECES):
        wait_bytes(others(xs, p), x_recv.at[p])

        def rotate(step, carry):
            at = pl.multiple_of(p * piece + step * STEP, STEP)
            here = pl.multiple_of(my_row + at, STEP)
            spec = [xs[s, pl.ds(at, STEP), :].astype(F32) for s in range(n)]
            cosine = [table_ref[pl.ds(here, STEP), b : b + 1] for b in range(sections)]
            sine = [
                table_ref[pl.ds(here, STEP), sections + b : sections + b + 1]
                for b in range(sections)
            ]

            def section(spec, b, flip):
                plus, minus = (sine[b], -sine[b]) if flip > 0 else (-sine[b], sine[b])
                return [
                    cosine[b] * spec[s] + (minus if s >> b & 1 else plus) * spec[s ^ (1 << b)]
                    for s in range(n)
                ]

            for b in range(sections):
                spec = section(spec, b, 1)
            spec = [spec[s] * fs[s, pl.ds(at, STEP), :].astype(F32) for s in range(n)]
            for b in reversed(range(sections)):
                spec = section(spec, b, -1)
            yr[0, pl.ds(here, STEP), :] = spec[0].astype(BF16)
            for s in range(1, n):
                ysend[s, pl.ds(at, STEP), :] = spec[s].astype(BF16)
            return carry

        lax.fori_loop(0, piece // STEP, rotate, 0)
        for s in range(n - 1, 0, -1):
            pltpu.make_async_remote_copy(
                src_ref=ysend.at[s, pl.ds(p * piece, piece)],
                dst_ref=yr.at[
                    s % lane_groups, pl.ds(pl.multiple_of(my_row + p * piece, STEP), piece)
                ],
                send_sem=y_send.at[p],
                recv_sem=y_recv.at[s],
                device_id={"seq": me ^ s},
                device_id_type=MESH,
            ).start()

    gate_copy.wait()

    def synthesise(t, carry):
        @pl.when(t > 0)
        def _():
            wait_bytes(ysend.at[t], y_recv.at[t])

        for u in range(1, row_groups):
            wait_bytes(ysend.at[u * lane_groups + t], y_recv.at[u * lane_groups + t])
        lanes = pl.ds(
            pl.multiple_of((lax.rem(me, lane_groups) ^ t) * LANES, LANES), LANES
        )
        back = [yr[t, pl.ds(k * blk, blk), :].astype(F32) for k in range(nb)]
        for k in range(nb):
            at = nb * nb + k * nb
            total = mix_ref[:, at : at + 1] * back[0]
            for other in range(1, nb):
                total += mix_ref[:, at + other : at + other + 1] * back[other]
            conv = jnp.dot(synthesis_ref[k], total.astype(BF16), preferred_element_type=F32)
            gated[pl.ds(k * blk, blk), lanes] = (
                gate_out[pl.ds(k * blk, blk), lanes].astype(F32) * conv
            ).astype(BF16)
        return carry

    lax.fori_loop(0, lane_groups, synthesise, 0)
    weight_copy.wait()

    share = tokens // 4
    blocks = weight.shape[1] // COLS

    def columns(q):
        return pl.ds(pl.multiple_of(q * COLS, COLS), COLS)

    def to_core(q):
        return pltpu.make_async_remote_copy(
            src_ref=part.at[q, 1 - core],
            dst_ref=first.at[q],
            send_sem=first_send_sem.at[q],
            recv_sem=first_recv_sem.at[q],
            device_id={"chan": core_peer},
            device_id_type=MESH,
        )

    def to_side(q):
        return pltpu.make_async_remote_copy(
            src_ref=second_send.at[q],
            dst_ref=second.at[q],
            send_sem=second_send_sem.at[q],
            recv_sem=second_recv_sem.at[q],
            device_id={"chan": side_peer},
            device_id_type=MESH,
        )

    def forward(q):
        to_core(q).wait_recv()
        second_send[q] = (
            part[q, core, 1 - side].astype(F32) + first[q, 1 - side].astype(F32)
        ).astype(BF16)
        to_side(q).start()

    def project(q, carry):
        product = jnp.dot(gated[...], weight[:, columns(q)], preferred_element_type=F32)
        for g in range(4):
            part[q, g % 2, g // 2] = product[g * share : (g + 1) * share].astype(BF16)
        to_core(q).start()

        @pl.when(q > 0)
        def _():
            forward(q - 1)

        return carry

    lax.fori_loop(0, blocks, project, 0)
    forward(blocks - 1)

    def finish(q, carry):
        to_side(q).wait_recv()
        out_ref[:, columns(q)] = (
            part[q, core, side].astype(F32)
            + first[q, side].astype(F32)
            + second[q].astype(F32)
        ).astype(BF16)
        to_core(q).wait_send()
        to_side(q).wait_send()
        return carry

    lax.fori_loop(0, blocks, finish, 0)
    wait_bytes(fs.at[pl.ds(1, n - 1)], f_send)
    for p in range(PIECES):
        wait_bytes(others(xs, p), x_send.at[p])
        wait_bytes(others(ysend, p), y_send.at[p])


def per_device(
    value_in,
    gate_in,
    gate_out,
    spectral_filter,
    analysis_blocks,
    analysis_mix,
    synthesis_blocks,
    synthesis_mix,
    angles,
    out_weight,
):
    tokens, chans = value_in.shape
    analysis_mix = analysis_mix.transpose(1, 2, 0)
    synthesis_mix = synthesis_mix.transpose(1, 2, 0)
    blk = analysis_blocks.shape[1]
    width = out_weight.shape[1]
    n = lax.axis_size("seq")
    lane_groups = min(n, chans // LANES)
    rows = tokens // (n // lane_groups)
    blocks = width // COLS
    share = tokens // 4
    vmem = pl.BlockSpec(memory_space=pltpu.VMEM)
    hbm = pl.BlockSpec(memory_space=pltpu.HBM)
    chunk = pltpu.VMEM((n, rows, LANES), BF16)
    whole = pltpu.VMEM((lane_groups, tokens, LANES), BF16)
    return pl.pallas_call(
        functools.partial(kernel, n, lane_groups),
        out_shape=jax.ShapeDtypeStruct((share, width), BF16),
        in_specs=[hbm] * 10,
        out_specs=vmem,
        scratch_shapes=[
            pltpu.VMEM((tokens, chans), BF16),
            pltpu.VMEM((tokens, chans), BF16),
            pltpu.VMEM(analysis_blocks.shape, BF16),
            pltpu.VMEM(synthesis_blocks.shape, BF16),
            pltpu.VMEM(analysis_mix.shape, BF16),
            pltpu.VMEM(synthesis_mix.shape, BF16),
            pltpu.VMEM(angles.shape, F32),
            pltpu.VMEM((blk, LANES), F32),
            pltpu.VMEM((tokens, LANES), F32),
            pltpu.VMEM((LANES, blk), F32),
            whole,
            chunk,
            chunk,
            chunk,
            whole,
            pltpu.VMEM((tokens, chans), BF16),
            pltpu.VMEM(out_weight.shape, BF16),
            pltpu.VMEM((tokens, chans), BF16),
            pltpu.VMEM((blocks, 2, 2, share, COLS), BF16),
            pltpu.VMEM((blocks, 2, share, COLS), BF16),
            pltpu.VMEM((blocks, share, COLS), BF16),
            pltpu.VMEM((blocks, share, COLS), BF16),
            pltpu.SemaphoreType.DMA,
            pltpu.SemaphoreType.DMA,
            pltpu.SemaphoreType.DMA((PIECES,)),
            pltpu.SemaphoreType.DMA((PIECES,)),
            pltpu.SemaphoreType.DMA((PIECES,)),
            pltpu.SemaphoreType.DMA((n,)),
            pltpu.SemaphoreType.DMA((3,)),
            pltpu.SemaphoreType.DMA((7,)),
            pltpu.SemaphoreType.DMA((blocks,)),
            pltpu.SemaphoreType.DMA((blocks,)),
            pltpu.SemaphoreType.DMA((blocks,)),
            pltpu.SemaphoreType.DMA((blocks,)),
        ],
        compiler_params=pltpu.CompilerParams(
            collective_id=0, has_side_effects=True, vmem_limit_bytes=62 * 2**20
        ),
    )(
        value_in,
        gate_in,
        spectral_filter,
        gate_out,
        analysis_blocks,
        synthesis_blocks,
        analysis_mix,
        synthesis_mix,
        angles,
        out_weight,
    )


def solution(mesh):
    placed = (
        P("seq", "chan"),
        P("seq", "chan"),
        P("seq", "chan"),
        P("seq", "chan"),
        P(),
        P(),
        P(),
        P(),
        P(),
        P("chan", None),
    )
    return jax.shard_map(
        per_device, mesh=mesh, in_specs=placed, out_specs=P(("seq", "chan"), None), check_vma=False
    )
```

```python
import functools

import jax
import jax.numpy as jnp
from jax import lax
from jax.experimental import pallas as pl
from jax.experimental.pallas import tpu as pltpu
from jax.sharding import PartitionSpec as P

MESH = pl.DeviceIdType.MESH
LANES = 128
PIECES = 3
STEP = 16
COLS = 256
F32 = jnp.float32
BF16 = jnp.bfloat16


def kernel(
    n,
    lane_groups,
    value_hbm,
    gate_hbm,
    filter_ref,
    gate_out_ref,
    analysis_hbm,
    synthesis_hbm,
    analysis_mix_hbm,
    synthesis_mix_hbm,
    angles_hbm,
    weight_ref,
    own_ref,
    second,
    value_ref,
    gate_ref,
    analysis_ref,
    synthesis_ref,
    analysis_mix,
    synthesis_mix,
    angles,
    mix_ref,
    table_ref,
    wide,
    xsend,
    xs,
    fs,
    ysend,
    yr,
    gate_out,
    weight,
    gated,
    part,
    first,
    second_send,
    own,
    f_send,
    f_recv,
    x_send,
    x_recv,
    y_send,
    y_recv,
    local_sem,
    load_sem,
    first_send_sem,
    first_recv_sem,
    second_send_sem,
    second_recv_sem,
    own_sem,
):
    me = lax.axis_index("seq")
    chan = lax.axis_index("chan")
    core = lax.rem(chan, 2)
    side = chan // 2
    core_peer = chan + 1 - 2 * core
    side_peer = (1 - side) * 2 + core
    tokens = value_hbm.shape[0]
    nb, blk, _ = analysis_hbm.shape
    row_groups = n // lane_groups
    rows = tokens // row_groups
    piece = rows // PIECES
    sections = n.bit_length() - 1

    loads = [
        pltpu.make_async_copy(source, target, load_sem.at[at])
        for at, (source, target) in enumerate(
            (
                (value_hbm, value_ref),
                (gate_hbm, gate_ref),
                (analysis_hbm, analysis_ref),
                (analysis_mix_hbm, analysis_mix),
                (synthesis_mix_hbm, synthesis_mix),
                (angles_hbm, angles),
                (synthesis_hbm, synthesis_ref),
            )
        )
    ]
    for load in loads:
        load.start()

    barrier = pltpu.get_barrier_semaphore()
    for s in range(1, n):
        pl.semaphore_signal(barrier, inc=1, device_id={"seq": me ^ s}, device_id_type=MESH)
    pl.semaphore_signal(barrier, inc=1, device_id={"chan": core_peer}, device_id_type=MESH)
    pl.semaphore_signal(barrier, inc=1, device_id={"chan": side_peer}, device_id_type=MESH)
    pl.semaphore_wait(barrier, n + 1)

    def chunk_lanes(index):
        return pl.ds(pl.multiple_of(lax.rem(index, lane_groups) * LANES, LANES), LANES)

    def chunk_row(index):
        return pl.multiple_of((index // lane_groups) * rows, STEP)

    my_row = chunk_row(me)

    for s in range(n - 1, 0, -1):
        there = me ^ s
        pltpu.make_async_remote_copy(
            src_ref=filter_ref.at[pl.ds(chunk_row(there), rows), chunk_lanes(there)],
            dst_ref=fs.at[s],
            send_sem=f_send,
            recv_sem=f_recv,
            device_id={"seq": there},
            device_id_type=MESH,
        ).start()
    own_filter = pltpu.make_async_copy(
        filter_ref.at[pl.ds(my_row, rows), chunk_lanes(me)], fs.at[0], local_sem.at[0]
    )
    own_filter.start()
    weight_copy = pltpu.make_async_copy(weight_ref, weight, local_sem.at[1])
    weight_copy.start()
    gate_copy = pltpu.make_async_copy(gate_out_ref, gate_out, local_sem.at[2])
    gate_copy.start()

    for load in loads:
        load.wait()

    wide[...] = jnp.zeros_like(wide)
    for which, source in enumerate((analysis_mix, synthesis_mix)):
        for k in range(nb):
            at = (which * nb + k) * nb
            wide[pl.ds(at, nb), :] = source[k].astype(F32)
    mix_ref[...] = wide[...].T

    def analyse(step, carry):
        t = lane_groups - 1 - step
        lanes = pl.ds(
            pl.multiple_of((lax.rem(me, lane_groups) ^ t) * LANES, LANES), LANES
        )
        mixed = (gate_ref[:, lanes].astype(F32) * value_ref[:, lanes].astype(F32)).astype(BF16)
        inner = [
            jnp.dot(
                analysis_ref[k], mixed[k * blk : (k + 1) * blk], preferred_element_type=F32
            )
            .astype(BF16)
            .astype(F32)
            for k in range(nb)
        ]
        for k in range(nb):
            total = mix_ref[:, k * nb : k * nb + 1] * inner[0]
            for other in range(1, nb):
                at = k * nb + other
                total += mix_ref[:, at : at + 1] * inner[other]
            xsend[t, pl.ds(k * blk, blk), :] = total.astype(BF16)
        return carry

    lax.fori_loop(0, lane_groups, analyse, 0)
    xs[0] = xsend[0, pl.ds(my_row, rows), :]
    for p in range(PIECES):
        for s in range(n - 1, 0, -1):
            there = me ^ s
            pltpu.make_async_remote_copy(
                src_ref=xsend.at[
                    s % lane_groups,
                    pl.ds(pl.multiple_of(chunk_row(there) + p * piece, STEP), piece),
                ],
                dst_ref=xs.at[s, pl.ds(p * piece, piece)],
                send_sem=x_send.at[p],
                recv_sem=x_recv.at[p],
                device_id={"seq": there},
                device_id_type=MESH,
            ).start()

    for k in range(nb):
        theta = angles[:, pl.ds(k * blk, blk)]
        cosine, sine = jnp.cos(theta), jnp.sin(theta)
        for b in range(sections):
            sign = (1 - 2 * (me >> b & 1)).astype(F32)
            wide[pl.ds(b, 1), :] = cosine[b : b + 1]
            wide[pl.ds(sections + b, 1), :] = sine[b : b + 1] * sign
        table_ref[pl.ds(k * blk, blk), :] = wide[...].T

    def others(ref, p):
        return ref.at[pl.ds(1, n - 1), pl.ds(p * piece, piece)]

    def wait_bytes(ref, sem):
        pltpu.make_async_copy(ref, ref, sem).wait()

    own_filter.wait()
    wait_bytes(fs.at[pl.ds(1, n - 1)], f_recv)
    for p in range(PIECES):
        wait_bytes(others(xs, p), x_recv.at[p])

        def rotate(step, carry):
            at = pl.multiple_of(p * piece + step * STEP, STEP)
            here = pl.multiple_of(my_row + at, STEP)
            spec = [xs[s, pl.ds(at, STEP), :].astype(F32) for s in range(n)]
            cosine = [table_ref[pl.ds(here, STEP), b : b + 1] for b in range(sections)]
            sine = [
                table_ref[pl.ds(here, STEP), sections + b : sections + b + 1]
                for b in range(sections)
            ]

            def section(spec, b, flip):
                plus, minus = (sine[b], -sine[b]) if flip > 0 else (-sine[b], sine[b])
                return [
                    cosine[b] * spec[s] + (minus if s >> b & 1 else plus) * spec[s ^ (1 << b)]
                    for s in range(n)
                ]

            for b in range(sections):
                spec = section(spec, b, 1)
            spec = [spec[s] * fs[s, pl.ds(at, STEP), :].astype(F32) for s in range(n)]
            for b in reversed(range(sections)):
                spec = section(spec, b, -1)
            yr[0, pl.ds(here, STEP), :] = spec[0].astype(BF16)
            for s in range(1, n):
                ysend[s, pl.ds(at, STEP), :] = spec[s].astype(BF16)
            return carry

        lax.fori_loop(0, piece // STEP, rotate, 0)
        for s in range(n - 1, 0, -1):
            pltpu.make_async_remote_copy(
                src_ref=ysend.at[s, pl.ds(p * piece, piece)],
                dst_ref=yr.at[
                    s % lane_groups, pl.ds(pl.multiple_of(my_row + p * piece, STEP), piece)
                ],
                send_sem=y_send.at[p],
                recv_sem=y_recv.at[s],
                device_id={"seq": me ^ s},
                device_id_type=MESH,
            ).start()

    gate_copy.wait()

    def synthesise(t, carry):
        @pl.when(t > 0)
        def _():
            wait_bytes(ysend.at[t], y_recv.at[t])

        for u in range(1, row_groups):
            wait_bytes(ysend.at[u * lane_groups + t], y_recv.at[u * lane_groups + t])
        lanes = pl.ds(
            pl.multiple_of((lax.rem(me, lane_groups) ^ t) * LANES, LANES), LANES
        )
        back = [yr[t, pl.ds(k * blk, blk), :].astype(F32) for k in range(nb)]
        for k in range(nb):
            at = nb * nb + k * nb
            total = mix_ref[:, at : at + 1] * back[0]
            for other in range(1, nb):
                total += mix_ref[:, at + other : at + other + 1] * back[other]
            conv = jnp.dot(synthesis_ref[k], total.astype(BF16), preferred_element_type=F32)
            gated[pl.ds(k * blk, blk), lanes] = (
                gate_out[pl.ds(k * blk, blk), lanes].astype(F32) * conv
            ).astype(BF16)
        return carry

    lax.fori_loop(0, lane_groups, synthesise, 0)
    weight_copy.wait()

    share = tokens // 4
    blocks = weight.shape[1] // COLS

    def columns(q):
        return pl.ds(pl.multiple_of(q * COLS, COLS), COLS)

    def to_core(q):
        return pltpu.make_async_remote_copy(
            src_ref=part.at[q, 1 - core],
            dst_ref=first.at[q],
            send_sem=first_send_sem.at[q],
            recv_sem=first_recv_sem.at[q],
            device_id={"chan": core_peer},
            device_id_type=MESH,
        )

    def to_side(q):
        return pltpu.make_async_remote_copy(
            src_ref=second_send.at[q],
            dst_ref=second.at[:, columns(q)],
            send_sem=second_send_sem.at[q],
            recv_sem=second_recv_sem.at[q],
            device_id={"chan": side_peer},
            device_id_type=MESH,
        )

    def keep(q):
        return pltpu.make_async_copy(own.at[q], own_ref.at[:, columns(q)], own_sem.at[q])

    def forward(q):
        to_core(q).wait_recv()
        second_send[q] = (
            part[q, core, 1 - side].astype(F32) + first[q, 1 - side].astype(F32)
        ).astype(BF16)
        to_side(q).start()
        own[q] = (part[q, core, side].astype(F32) + first[q, side].astype(F32)).astype(BF16)
        keep(q).start()

    def project(q, carry):
        product = jnp.dot(gated[...], weight[:, columns(q)], preferred_element_type=F32)
        for g in range(4):
            part[q, g % 2, g // 2] = product[g * share : (g + 1) * share].astype(BF16)
        to_core(q).start()

        @pl.when(q > 0)
        def _():
            forward(q - 1)

        return carry

    lax.fori_loop(0, blocks, project, 0)
    forward(blocks - 1)

    def finish(q, carry):
        to_side(q).wait_recv()
        keep(q).wait()
        to_core(q).wait_send()
        to_side(q).wait_send()
        return carry

    lax.fori_loop(0, blocks, finish, 0)
    wait_bytes(fs.at[pl.ds(1, n - 1)], f_send)
    for p in range(PIECES):
        wait_bytes(others(xs, p), x_send.at[p])
        wait_bytes(others(ysend, p), y_send.at[p])


def per_device(
    value_in,
    gate_in,
    gate_out,
    spectral_filter,
    analysis_blocks,
    analysis_mix,
    synthesis_blocks,
    synthesis_mix,
    angles,
    out_weight,
):
    tokens, chans = value_in.shape
    analysis_mix = analysis_mix.transpose(1, 2, 0)
    synthesis_mix = synthesis_mix.transpose(1, 2, 0)
    blk = analysis_blocks.shape[1]
    width = out_weight.shape[1]
    n = lax.axis_size("seq")
    lane_groups = min(n, chans // LANES)
    rows = tokens // (n // lane_groups)
    blocks = width // COLS
    share = tokens // 4
    hbm = pl.BlockSpec(memory_space=pltpu.HBM)
    chunk = pltpu.VMEM((n, rows, LANES), BF16)
    whole = pltpu.VMEM((lane_groups, tokens, LANES), BF16)
    own, other = pl.pallas_call(
        functools.partial(kernel, n, lane_groups),
        out_shape=[jax.ShapeDtypeStruct((share, width), BF16)] * 2,
        in_specs=[hbm] * 10,
        out_specs=[hbm] * 2,
        scratch_shapes=[
            pltpu.VMEM((tokens, chans), BF16),
            pltpu.VMEM((tokens, chans), BF16),
            pltpu.VMEM(analysis_blocks.shape, BF16),
            pltpu.VMEM(synthesis_blocks.shape, BF16),
            pltpu.VMEM(analysis_mix.shape, BF16),
            pltpu.VMEM(synthesis_mix.shape, BF16),
            pltpu.VMEM(angles.shape, F32),
            pltpu.VMEM((blk, LANES), F32),
            pltpu.VMEM((tokens, LANES), F32),
            pltpu.VMEM((LANES, blk), F32),
            whole,
            chunk,
            chunk,
            chunk,
            whole,
            pltpu.VMEM((tokens, chans), BF16),
            pltpu.VMEM(out_weight.shape, BF16),
            pltpu.VMEM((tokens, chans), BF16),
            pltpu.VMEM((blocks, 2, 2, share, COLS), BF16),
            pltpu.VMEM((blocks, 2, share, COLS), BF16),
            pltpu.VMEM((blocks, share, COLS), BF16),
            pltpu.VMEM((blocks, share, COLS), BF16),
            pltpu.SemaphoreType.DMA,
            pltpu.SemaphoreType.DMA,
            pltpu.SemaphoreType.DMA((PIECES,)),
            pltpu.SemaphoreType.DMA((PIECES,)),
            pltpu.SemaphoreType.DMA((PIECES,)),
            pltpu.SemaphoreType.DMA((n,)),
            pltpu.SemaphoreType.DMA((3,)),
            pltpu.SemaphoreType.DMA((7,)),
            pltpu.SemaphoreType.DMA((blocks,)),
            pltpu.SemaphoreType.DMA((blocks,)),
            pltpu.SemaphoreType.DMA((blocks,)),
            pltpu.SemaphoreType.DMA((blocks,)),
            pltpu.SemaphoreType.DMA((blocks,)),
        ],
        compiler_params=pltpu.CompilerParams(
            collective_id=0, has_side_effects=True, vmem_limit_bytes=62 * 2**20
        ),
    )(
        value_in,
        gate_in,
        spectral_filter,
        gate_out,
        analysis_blocks,
        synthesis_blocks,
        analysis_mix,
        synthesis_mix,
        angles,
        out_weight,
    )
    return (own.astype(F32) + other.astype(F32)).astype(BF16)


def solution(mesh):
    placed = (
        P("seq", "chan"),
        P("seq", "chan"),
        P("seq", "chan"),
        P("seq", "chan"),
        P(),
        P(),
        P(),
        P(),
        P(),
        P("chan", None),
    )
    return jax.shard_map(
        per_device, mesh=mesh, in_specs=placed, out_specs=P(("seq", "chan"), None), check_vma=False
    )
```

```python
import functools

import jax
import jax.numpy as jnp
from jax import lax
from jax.experimental import pallas as pl
from jax.experimental.pallas import tpu as pltpu
from jax.sharding import PartitionSpec as P

MESH = pl.DeviceIdType.MESH
LANES = 128
PIECES = 3
STEP = 16
COLS = 512
F32 = jnp.float32
BF16 = jnp.bfloat16


def kernel(
    n,
    lane_groups,
    value_hbm,
    gate_hbm,
    filter_ref,
    gate_out_ref,
    analysis_hbm,
    synthesis_hbm,
    analysis_mix_hbm,
    synthesis_mix_hbm,
    angles_hbm,
    weight_ref,
    out_ref,
    value_ref,
    gate_ref,
    analysis_ref,
    synthesis_ref,
    analysis_mix,
    synthesis_mix,
    angles,
    mix_ref,
    table_ref,
    wide,
    xsend,
    xs,
    fs,
    ysend,
    yr,
    gate_out,
    weight,
    gated,
    part,
    first,
    second_send,
    second,
    f_send,
    f_recv,
    x_send,
    x_recv,
    y_send,
    y_recv,
    local_sem,
    load_sem,
    first_send_sem,
    first_recv_sem,
    second_send_sem,
    second_recv_sem,
):
    me = lax.axis_index("seq")
    chan = lax.axis_index("chan")
    core = lax.rem(chan, 2)
    side = chan // 2
    core_peer = chan + 1 - 2 * core
    side_peer = (1 - side) * 2 + core
    tokens = value_hbm.shape[0]
    nb, blk, _ = analysis_hbm.shape
    row_groups = n // lane_groups
    rows = tokens // row_groups
    piece = rows // PIECES
    sections = n.bit_length() - 1

    loads = [
        pltpu.make_async_copy(source, target, load_sem.at[at])
        for at, (source, target) in enumerate(
            (
                (value_hbm, value_ref),
                (gate_hbm, gate_ref),
                (analysis_hbm, analysis_ref),
                (analysis_mix_hbm, analysis_mix),
                (synthesis_mix_hbm, synthesis_mix),
                (angles_hbm, angles),
                (synthesis_hbm, synthesis_ref),
            )
        )
    ]
    for load in loads:
        load.start()

    order = [
        s
        for step in range(n // 2)
        for s in (n - 1 - step, n // 2 - 1 - step)
        if s > 0
    ]

    barrier = pltpu.get_barrier_semaphore()
    for s in range(1, n):
        pl.semaphore_signal(barrier, inc=1, device_id={"seq": me ^ s}, device_id_type=MESH)
    pl.semaphore_signal(barrier, inc=1, device_id={"chan": core_peer}, device_id_type=MESH)
    pl.semaphore_signal(barrier, inc=1, device_id={"chan": side_peer}, device_id_type=MESH)
    pl.semaphore_wait(barrier, n + 1)

    def chunk_lanes(index):
        return pl.ds(pl.multiple_of(lax.rem(index, lane_groups) * LANES, LANES), LANES)

    def chunk_row(index):
        return pl.multiple_of((index // lane_groups) * rows, STEP)

    my_row = chunk_row(me)

    for s in order:
        there = me ^ s
        pltpu.make_async_remote_copy(
            src_ref=filter_ref.at[pl.ds(chunk_row(there), rows), chunk_lanes(there)],
            dst_ref=fs.at[s],
            send_sem=f_send,
            recv_sem=f_recv,
            device_id={"seq": there},
            device_id_type=MESH,
        ).start()
    own_filter = pltpu.make_async_copy(
        filter_ref.at[pl.ds(my_row, rows), chunk_lanes(me)], fs.at[0], local_sem.at[0]
    )
    own_filter.start()
    weight_copy = pltpu.make_async_copy(weight_ref, weight, local_sem.at[1])
    weight_copy.start()
    gate_copy = pltpu.make_async_copy(gate_out_ref, gate_out, local_sem.at[2])
    gate_copy.start()

    for load in loads:
        load.wait()

    wide[...] = jnp.zeros_like(wide)
    for which, source in enumerate((analysis_mix, synthesis_mix)):
        for k in range(nb):
            at = (which * nb + k) * nb
            wide[pl.ds(at, nb), :] = source[k].astype(F32)
    mix_ref[...] = wide[...].T

    def analyse(step, carry):
        t = lane_groups - 1 - step
        lanes = pl.ds(
            pl.multiple_of((lax.rem(me, lane_groups) ^ t) * LANES, LANES), LANES
        )
        mixed = (gate_ref[:, lanes].astype(F32) * value_ref[:, lanes].astype(F32)).astype(BF16)
        inner = [
            jnp.dot(
                analysis_ref[k], mixed[k * blk : (k + 1) * blk], preferred_element_type=F32
            )
            .astype(BF16)
            .astype(F32)
            for k in range(nb)
        ]
        for k in range(nb):
            total = mix_ref[:, k * nb : k * nb + 1] * inner[0]
            for other in range(1, nb):
                at = k * nb + other
                total += mix_ref[:, at : at + 1] * inner[other]
            xsend[t, pl.ds(k * blk, blk), :] = total.astype(BF16)
        return carry

    lax.fori_loop(0, lane_groups, analyse, 0)
    xs[0] = xsend[0, pl.ds(my_row, rows), :]
    for p in range(PIECES):
        for s in order:
            there = me ^ s
            pltpu.make_async_remote_copy(
                src_ref=xsend.at[
                    s % lane_groups,
                    pl.ds(pl.multiple_of(chunk_row(there) + p * piece, STEP), piece),
                ],
                dst_ref=xs.at[s, pl.ds(p * piece, piece)],
                send_sem=x_send.at[p],
                recv_sem=x_recv.at[p],
                device_id={"seq": there},
                device_id_type=MESH,
            ).start()

    for k in range(nb):
        theta = angles[:, pl.ds(k * blk, blk)]
        cosine, sine = jnp.cos(theta), jnp.sin(theta)
        for b in range(sections):
            sign = (1 - 2 * (me >> b & 1)).astype(F32)
            wide[pl.ds(b, 1), :] = cosine[b : b + 1]
            wide[pl.ds(sections + b, 1), :] = sine[b : b + 1] * sign
        table_ref[pl.ds(k * blk, blk), :] = wide[...].T

    def others(ref, p):
        return ref.at[pl.ds(1, n - 1), pl.ds(p * piece, piece)]

    def wait_bytes(ref, sem):
        pltpu.make_async_copy(ref, ref, sem).wait()

    own_filter.wait()
    wait_bytes(fs.at[pl.ds(1, n - 1)], f_recv)
    for p in range(PIECES):
        wait_bytes(others(xs, p), x_recv.at[p])

        def rotate(step, carry):
            at = pl.multiple_of(p * piece + step * STEP, STEP)
            here = pl.multiple_of(my_row + at, STEP)
            spec = [xs[s, pl.ds(at, STEP), :].astype(F32) for s in range(n)]
            cosine = [table_ref[pl.ds(here, STEP), b : b + 1] for b in range(sections)]
            sine = [
                table_ref[pl.ds(here, STEP), sections + b : sections + b + 1]
                for b in range(sections)
            ]

            def section(spec, b, flip):
                plus, minus = (sine[b], -sine[b]) if flip > 0 else (-sine[b], sine[b])
                return [
                    cosine[b] * spec[s] + (minus if s >> b & 1 else plus) * spec[s ^ (1 << b)]
                    for s in range(n)
                ]

            for b in range(sections):
                spec = section(spec, b, 1)
            spec = [spec[s] * fs[s, pl.ds(at, STEP), :].astype(F32) for s in range(n)]
            for b in reversed(range(sections)):
                spec = section(spec, b, -1)
            yr[0, pl.ds(here, STEP), :] = spec[0].astype(BF16)
            for s in range(1, n):
                ysend[s, pl.ds(at, STEP), :] = spec[s].astype(BF16)
            return carry

        lax.fori_loop(0, piece // STEP, rotate, 0)
        for s in order:
            pltpu.make_async_remote_copy(
                src_ref=ysend.at[s, pl.ds(p * piece, piece)],
                dst_ref=yr.at[
                    s % lane_groups, pl.ds(pl.multiple_of(my_row + p * piece, STEP), piece)
                ],
                send_sem=y_send.at[p],
                recv_sem=y_recv.at[s],
                device_id={"seq": me ^ s},
                device_id_type=MESH,
            ).start()

    gate_copy.wait()

    def synthesise(t, carry):
        @pl.when(t > 0)
        def _():
            wait_bytes(ysend.at[t], y_recv.at[t])

        for u in range(1, row_groups):
            wait_bytes(ysend.at[u * lane_groups + t], y_recv.at[u * lane_groups + t])
        lanes = pl.ds(
            pl.multiple_of((lax.rem(me, lane_groups) ^ t) * LANES, LANES), LANES
        )
        back = [yr[t, pl.ds(k * blk, blk), :].astype(F32) for k in range(nb)]
        for k in range(nb):
            at = nb * nb + k * nb
            total = mix_ref[:, at : at + 1] * back[0]
            for other in range(1, nb):
                total += mix_ref[:, at + other : at + other + 1] * back[other]
            conv = jnp.dot(synthesis_ref[k], total.astype(BF16), preferred_element_type=F32)
            gated[pl.ds(k * blk, blk), lanes] = (
                gate_out[pl.ds(k * blk, blk), lanes].astype(F32) * conv
            ).astype(BF16)
        return carry

    lax.fori_loop(0, lane_groups, synthesise, 0)
    weight_copy.wait()

    share = tokens // 4
    blocks = weight.shape[1] // COLS

    def columns(q):
        return pl.ds(pl.multiple_of(q * COLS, COLS), COLS)

    def to_core(q):
        return pltpu.make_async_remote_copy(
            src_ref=part.at[q, 1 - core],
            dst_ref=first.at[q],
            send_sem=first_send_sem.at[q],
            recv_sem=first_recv_sem.at[q],
            device_id={"chan": core_peer},
            device_id_type=MESH,
        )

    def to_side(q):
        return pltpu.make_async_remote_copy(
            src_ref=second_send.at[q],
            dst_ref=second.at[q],
            send_sem=second_send_sem.at[q],
            recv_sem=second_recv_sem.at[q],
            device_id={"chan": side_peer},
            device_id_type=MESH,
        )

    def forward(q):
        to_core(q).wait_recv()
        second_send[q] = (
            part[q, core, 1 - side].astype(F32) + first[q, 1 - side].astype(F32)
        ).astype(BF16)
        to_side(q).start()

    def project(q, carry):
        product = jnp.dot(gated[...], weight[:, columns(q)], preferred_element_type=F32)
        for g in range(4):
            part[q, g % 2, g // 2] = product[g * share : (g + 1) * share].astype(BF16)
        to_core(q).start()

        @pl.when(q > 0)
        def _():
            forward(q - 1)

        return carry

    lax.fori_loop(0, blocks, project, 0)
    forward(blocks - 1)

    def finish(q, carry):
        to_side(q).wait_recv()
        out_ref[:, columns(q)] = (
            part[q, core, side].astype(F32)
            + first[q, side].astype(F32)
            + second[q].astype(F32)
        ).astype(BF16)
        to_core(q).wait_send()
        to_side(q).wait_send()
        return carry

    lax.fori_loop(0, blocks, finish, 0)
    wait_bytes(fs.at[pl.ds(1, n - 1)], f_send)
    for p in range(PIECES):
        wait_bytes(others(xs, p), x_send.at[p])
        wait_bytes(others(ysend, p), y_send.at[p])


def per_device(
    value_in,
    gate_in,
    gate_out,
    spectral_filter,
    analysis_blocks,
    analysis_mix,
    synthesis_blocks,
    synthesis_mix,
    angles,
    out_weight,
):
    tokens, chans = value_in.shape
    analysis_mix = analysis_mix.transpose(1, 2, 0)
    synthesis_mix = synthesis_mix.transpose(1, 2, 0)
    blk = analysis_blocks.shape[1]
    width = out_weight.shape[1]
    n = lax.axis_size("seq")
    lane_groups = min(n, chans // LANES)
    rows = tokens // (n // lane_groups)
    blocks = width // COLS
    share = tokens // 4
    vmem = pl.BlockSpec(memory_space=pltpu.VMEM)
    hbm = pl.BlockSpec(memory_space=pltpu.HBM)
    chunk = pltpu.VMEM((n, rows, LANES), BF16)
    whole = pltpu.VMEM((lane_groups, tokens, LANES), BF16)
    return pl.pallas_call(
        functools.partial(kernel, n, lane_groups),
        out_shape=jax.ShapeDtypeStruct((share, width), BF16),
        in_specs=[hbm] * 10,
        out_specs=vmem,
        scratch_shapes=[
            pltpu.VMEM((tokens, chans), BF16),
            pltpu.VMEM((tokens, chans), BF16),
            pltpu.VMEM(analysis_blocks.shape, BF16),
            pltpu.VMEM(synthesis_blocks.shape, BF16),
            pltpu.VMEM(analysis_mix.shape, BF16),
            pltpu.VMEM(synthesis_mix.shape, BF16),
            pltpu.VMEM(angles.shape, F32),
            pltpu.VMEM((blk, LANES), F32),
            pltpu.VMEM((tokens, LANES), F32),
            pltpu.VMEM((LANES, blk), F32),
            whole,
            chunk,
            chunk,
            chunk,
            whole,
            pltpu.VMEM((tokens, chans), BF16),
            pltpu.VMEM(out_weight.shape, BF16),
            pltpu.VMEM((tokens, chans), BF16),
            pltpu.VMEM((blocks, 2, 2, share, COLS), BF16),
            pltpu.VMEM((blocks, 2, share, COLS), BF16),
            pltpu.VMEM((blocks, share, COLS), BF16),
            pltpu.VMEM((blocks, share, COLS), BF16),
            pltpu.SemaphoreType.DMA,
            pltpu.SemaphoreType.DMA,
            pltpu.SemaphoreType.DMA((PIECES,)),
            pltpu.SemaphoreType.DMA((PIECES,)),
            pltpu.SemaphoreType.DMA((PIECES,)),
            pltpu.SemaphoreType.DMA((n,)),
            pltpu.SemaphoreType.DMA((3,)),
            pltpu.SemaphoreType.DMA((7,)),
            pltpu.SemaphoreType.DMA((blocks,)),
            pltpu.SemaphoreType.DMA((blocks,)),
            pltpu.SemaphoreType.DMA((blocks,)),
            pltpu.SemaphoreType.DMA((blocks,)),
        ],
        compiler_params=pltpu.CompilerParams(
            collective_id=0, has_side_effects=True, vmem_limit_bytes=62 * 2**20
        ),
    )(
        value_in,
        gate_in,
        spectral_filter,
        gate_out,
        analysis_blocks,
        synthesis_blocks,
        analysis_mix,
        synthesis_mix,
        angles,
        out_weight,
    )


def solution(mesh):
    placed = (
        P("seq", "chan"),
        P("seq", "chan"),
        P("seq", "chan"),
        P("seq", "chan"),
        P(),
        P(),
        P(),
        P(),
        P(),
        P("chan", None),
    )
    return jax.shard_map(
        per_device, mesh=mesh, in_specs=placed, out_specs=P(("seq", "chan"), None), check_vma=False
    )
```

```python
import functools

import jax
import jax.numpy as jnp
from jax import lax
from jax.experimental import pallas as pl
from jax.experimental.pallas import tpu as pltpu
from jax.sharding import PartitionSpec as P

MESH = pl.DeviceIdType.MESH
LANES = 128
PIECES = 3
STEP = 16
COLS = 512
F32 = jnp.float32
BF16 = jnp.bfloat16


def kernel(
    n,
    lane_groups,
    value_hbm,
    gate_hbm,
    filter_ref,
    gate_out_ref,
    analysis_hbm,
    synthesis_hbm,
    analysis_mix_hbm,
    synthesis_mix_hbm,
    angles_hbm,
    weight_ref,
    out_ref,
    value_ref,
    gate_ref,
    analysis_ref,
    synthesis_ref,
    analysis_mix,
    synthesis_mix,
    angles,
    mix_ref,
    table_ref,
    wide,
    xsend,
    xs,
    fs,
    ysend,
    yr,
    gate_out,
    weight,
    gated,
    part,
    first,
    second_send,
    second,
    f_send,
    f_recv,
    x_send,
    x_recv,
    y_send,
    y_recv,
    local_sem,
    load_sem,
    first_send_sem,
    first_recv_sem,
    second_send_sem,
    second_recv_sem,
):
    me = lax.axis_index("seq")
    chan = lax.axis_index("chan")
    core = lax.rem(chan, 2)
    side = chan // 2
    core_peer = chan + 1 - 2 * core
    side_peer = (1 - side) * 2 + core
    tokens = value_hbm.shape[0]
    nb, blk, _ = analysis_hbm.shape
    row_groups = n // lane_groups
    rows = tokens // row_groups
    piece = rows // PIECES
    sections = n.bit_length() - 1

    loads = [
        pltpu.make_async_copy(source, target, load_sem.at[at])
        for at, (source, target) in enumerate(
            (
                (value_hbm, value_ref),
                (gate_hbm, gate_ref),
                (analysis_hbm, analysis_ref),
                (analysis_mix_hbm, analysis_mix),
                (synthesis_mix_hbm, synthesis_mix),
                (angles_hbm, angles),
                (synthesis_hbm, synthesis_ref),
            )
        )
    ]
    for load in loads:
        load.start()

    barrier = pltpu.get_barrier_semaphore()
    for s in range(1, n):
        pl.semaphore_signal(barrier, inc=1, device_id={"seq": me ^ s}, device_id_type=MESH)
    pl.semaphore_signal(barrier, inc=1, device_id={"chan": core_peer}, device_id_type=MESH)
    pl.semaphore_signal(barrier, inc=1, device_id={"chan": side_peer}, device_id_type=MESH)
    pl.semaphore_wait(barrier, n + 1)

    def chunk_lanes(index):
        return pl.ds(pl.multiple_of(lax.rem(index, lane_groups) * LANES, LANES), LANES)

    def chunk_row(index):
        return pl.multiple_of((index // lane_groups) * rows, STEP)

    my_row = chunk_row(me)

    for s in range(n - 1, 0, -1):
        there = me ^ s
        pltpu.make_async_remote_copy(
            src_ref=filter_ref.at[pl.ds(chunk_row(there), rows), chunk_lanes(there)],
            dst_ref=fs.at[s],
            send_sem=f_send,
            recv_sem=f_recv,
            device_id={"seq": there},
            device_id_type=MESH,
        ).start()
    own_filter = pltpu.make_async_copy(
        filter_ref.at[pl.ds(my_row, rows), chunk_lanes(me)], fs.at[0], local_sem.at[0]
    )
    own_filter.start()
    weight_copy = pltpu.make_async_copy(weight_ref, weight, local_sem.at[1])
    weight_copy.start()
    gate_copy = pltpu.make_async_copy(gate_out_ref, gate_out, local_sem.at[2])
    gate_copy.start()

    for load in loads:
        load.wait()

    wide[...] = jnp.zeros_like(wide)
    for which, source in enumerate((analysis_mix, synthesis_mix)):
        for k in range(nb):
            at = (which * nb + k) * nb
            wide[pl.ds(at, nb), :] = source[k].astype(F32)
    mix_ref[...] = wide[...].T

    def analyse(step, carry):
        t = lane_groups - 1 - step
        lanes = pl.ds(
            pl.multiple_of((lax.rem(me, lane_groups) ^ t) * LANES, LANES), LANES
        )
        mixed = (gate_ref[:, lanes].astype(F32) * value_ref[:, lanes].astype(F32)).astype(BF16)
        inner = [
            jnp.dot(
                analysis_ref[k], mixed[k * blk : (k + 1) * blk], preferred_element_type=F32
            )
            .astype(BF16)
            .astype(F32)
            for k in range(nb)
        ]
        for k in range(nb):
            total = mix_ref[:, k * nb : k * nb + 1] * inner[0]
            for other in range(1, nb):
                at = k * nb + other
                total += mix_ref[:, at : at + 1] * inner[other]
            xsend[t, pl.ds(k * blk, blk), :] = total.astype(BF16)
        return carry

    lax.fori_loop(0, lane_groups, analyse, 0)
    xs[0] = xsend[0, pl.ds(my_row, rows), :]

    def send_piece(p):
        for s in range(n - 1, 0, -1):
            there = me ^ s
            pltpu.make_async_remote_copy(
                src_ref=xsend.at[
                    s % lane_groups,
                    pl.ds(pl.multiple_of(chunk_row(there) + p * piece, STEP), piece),
                ],
                dst_ref=xs.at[s, pl.ds(p * piece, piece)],
                send_sem=x_send.at[p],
                recv_sem=x_recv.at[p],
                device_id={"seq": there},
                device_id_type=MESH,
            ).start()

    send_piece(0)
    for k in range(nb):
        theta = angles[:, pl.ds(k * blk, blk)]
        cosine, sine = jnp.cos(theta), jnp.sin(theta)
        for b in range(sections):
            sign = (1 - 2 * (me >> b & 1)).astype(F32)
            wide[pl.ds(b, 1), :] = cosine[b : b + 1]
            wide[pl.ds(sections + b, 1), :] = sine[b : b + 1] * sign
        table_ref[pl.ds(k * blk, blk), :] = wide[...].T

    def others(ref, p):
        return ref.at[pl.ds(1, n - 1), pl.ds(p * piece, piece)]

    def wait_bytes(ref, sem):
        pltpu.make_async_copy(ref, ref, sem).wait()

    own_filter.wait()
    wait_bytes(fs.at[pl.ds(1, n - 1)], f_recv)
    send_piece(1)
    for p in range(PIECES):
        wait_bytes(others(xs, p), x_recv.at[p])
        if p + 2 < PIECES:
            send_piece(p + 2)

        def rotate(step, carry):
            at = pl.multiple_of(p * piece + step * STEP, STEP)
            here = pl.multiple_of(my_row + at, STEP)
            spec = [xs[s, pl.ds(at, STEP), :].astype(F32) for s in range(n)]
            cosine = [table_ref[pl.ds(here, STEP), b : b + 1] for b in range(sections)]
            sine = [
                table_ref[pl.ds(here, STEP), sections + b : sections + b + 1]
                for b in range(sections)
            ]

            def section(spec, b, flip):
                plus, minus = (sine[b], -sine[b]) if flip > 0 else (-sine[b], sine[b])
                return [
                    cosine[b] * spec[s] + (minus if s >> b & 1 else plus) * spec[s ^ (1 << b)]
                    for s in range(n)
                ]

            for b in range(sections):
                spec = section(spec, b, 1)
            spec = [spec[s] * fs[s, pl.ds(at, STEP), :].astype(F32) for s in range(n)]
            for b in reversed(range(sections)):
                spec = section(spec, b, -1)
            yr[0, pl.ds(here, STEP), :] = spec[0].astype(BF16)
            for s in range(1, n):
                ysend[s, pl.ds(at, STEP), :] = spec[s].astype(BF16)
            return carry

        lax.fori_loop(0, piece // STEP, rotate, 0)
        for s in range(n - 1, 0, -1):
            pltpu.make_async_remote_copy(
                src_ref=ysend.at[s, pl.ds(p * piece, piece)],
                dst_ref=yr.at[
                    s % lane_groups, pl.ds(pl.multiple_of(my_row + p * piece, STEP), piece)
                ],
                send_sem=y_send.at[p],
                recv_sem=y_recv.at[s],
                device_id={"seq": me ^ s},
                device_id_type=MESH,
            ).start()

    gate_copy.wait()

    def synthesise(t, carry):
        @pl.when(t > 0)
        def _():
            wait_bytes(ysend.at[t], y_recv.at[t])

        for u in range(1, row_groups):
            wait_bytes(ysend.at[u * lane_groups + t], y_recv.at[u * lane_groups + t])
        lanes = pl.ds(
            pl.multiple_of((lax.rem(me, lane_groups) ^ t) * LANES, LANES), LANES
        )
        back = [yr[t, pl.ds(k * blk, blk), :].astype(F32) for k in range(nb)]
        for k in range(nb):
            at = nb * nb + k * nb
            total = mix_ref[:, at : at + 1] * back[0]
            for other in range(1, nb):
                total += mix_ref[:, at + other : at + other + 1] * back[other]
            conv = jnp.dot(synthesis_ref[k], total.astype(BF16), preferred_element_type=F32)
            gated[pl.ds(k * blk, blk), lanes] = (
                gate_out[pl.ds(k * blk, blk), lanes].astype(F32) * conv
            ).astype(BF16)
        return carry

    lax.fori_loop(0, lane_groups, synthesise, 0)
    weight_copy.wait()

    share = tokens // 4
    blocks = weight.shape[1] // COLS

    def columns(q):
        return pl.ds(pl.multiple_of(q * COLS, COLS), COLS)

    def to_core(q):
        return pltpu.make_async_remote_copy(
            src_ref=part.at[q, 1 - core],
            dst_ref=first.at[q],
            send_sem=first_send_sem.at[q],
            recv_sem=first_recv_sem.at[q],
            device_id={"chan": core_peer},
            device_id_type=MESH,
        )

    def to_side(q):
        return pltpu.make_async_remote_copy(
            src_ref=second_send.at[q],
            dst_ref=second.at[q],
            send_sem=second_send_sem.at[q],
            recv_sem=second_recv_sem.at[q],
            device_id={"chan": side_peer},
            device_id_type=MESH,
        )

    def forward(q):
        to_core(q).wait_recv()
        second_send[q] = (
            part[q, core, 1 - side].astype(F32) + first[q, 1 - side].astype(F32)
        ).astype(BF16)
        to_side(q).start()

    def project(q, carry):
        product = jnp.dot(gated[...], weight[:, columns(q)], preferred_element_type=F32)
        for g in range(4):
            part[q, g % 2, g // 2] = product[g * share : (g + 1) * share].astype(BF16)
        to_core(q).start()

        @pl.when(q > 0)
        def _():
            forward(q - 1)

        return carry

    lax.fori_loop(0, blocks, project, 0)
    forward(blocks - 1)

    def finish(q, carry):
        to_side(q).wait_recv()
        out_ref[:, columns(q)] = (
            part[q, core, side].astype(F32)
            + first[q, side].astype(F32)
            + second[q].astype(F32)
        ).astype(BF16)
        to_core(q).wait_send()
        to_side(q).wait_send()
        return carry

    lax.fori_loop(0, blocks, finish, 0)
    wait_bytes(fs.at[pl.ds(1, n - 1)], f_send)
    for p in range(PIECES):
        wait_bytes(others(xs, p), x_send.at[p])
        wait_bytes(others(ysend, p), y_send.at[p])


def per_device(
    value_in,
    gate_in,
    gate_out,
    spectral_filter,
    analysis_blocks,
    analysis_mix,
    synthesis_blocks,
    synthesis_mix,
    angles,
    out_weight,
):
    tokens, chans = value_in.shape
    analysis_mix = analysis_mix.transpose(1, 2, 0)
    synthesis_mix = synthesis_mix.transpose(1, 2, 0)
    blk = analysis_blocks.shape[1]
    width = out_weight.shape[1]
    n = lax.axis_size("seq")
    lane_groups = min(n, chans // LANES)
    rows = tokens // (n // lane_groups)
    blocks = width // COLS
    share = tokens // 4
    vmem = pl.BlockSpec(memory_space=pltpu.VMEM)
    hbm = pl.BlockSpec(memory_space=pltpu.HBM)
    chunk = pltpu.VMEM((n, rows, LANES), BF16)
    whole = pltpu.VMEM((lane_groups, tokens, LANES), BF16)
    return pl.pallas_call(
        functools.partial(kernel, n, lane_groups),
        out_shape=jax.ShapeDtypeStruct((share, width), BF16),
        in_specs=[hbm] * 10,
        out_specs=vmem,
        scratch_shapes=[
            pltpu.VMEM((tokens, chans), BF16),
            pltpu.VMEM((tokens, chans), BF16),
            pltpu.VMEM(analysis_blocks.shape, BF16),
            pltpu.VMEM(synthesis_blocks.shape, BF16),
            pltpu.VMEM(analysis_mix.shape, BF16),
            pltpu.VMEM(synthesis_mix.shape, BF16),
            pltpu.VMEM(angles.shape, F32),
            pltpu.VMEM((blk, LANES), F32),
            pltpu.VMEM((tokens, LANES), F32),
            pltpu.VMEM((LANES, blk), F32),
            whole,
            chunk,
            chunk,
            chunk,
            whole,
            pltpu.VMEM((tokens, chans), BF16),
            pltpu.VMEM(out_weight.shape, BF16),
            pltpu.VMEM((tokens, chans), BF16),
            pltpu.VMEM((blocks, 2, 2, share, COLS), BF16),
            pltpu.VMEM((blocks, 2, share, COLS), BF16),
            pltpu.VMEM((blocks, share, COLS), BF16),
            pltpu.VMEM((blocks, share, COLS), BF16),
            pltpu.SemaphoreType.DMA,
            pltpu.SemaphoreType.DMA,
            pltpu.SemaphoreType.DMA((PIECES,)),
            pltpu.SemaphoreType.DMA((PIECES,)),
            pltpu.SemaphoreType.DMA((PIECES,)),
            pltpu.SemaphoreType.DMA((n,)),
            pltpu.SemaphoreType.DMA((3,)),
            pltpu.SemaphoreType.DMA((7,)),
            pltpu.SemaphoreType.DMA((blocks,)),
            pltpu.SemaphoreType.DMA((blocks,)),
            pltpu.SemaphoreType.DMA((blocks,)),
            pltpu.SemaphoreType.DMA((blocks,)),
        ],
        compiler_params=pltpu.CompilerParams(
            collective_id=0, has_side_effects=True, vmem_limit_bytes=62 * 2**20
        ),
    )(
        value_in,
        gate_in,
        spectral_filter,
        gate_out,
        analysis_blocks,
        synthesis_blocks,
        analysis_mix,
        synthesis_mix,
        angles,
        out_weight,
    )


def solution(mesh):
    placed = (
        P("seq", "chan"),
        P("seq", "chan"),
        P("seq", "chan"),
        P("seq", "chan"),
        P(),
        P(),
        P(),
        P(),
        P(),
        P("chan", None),
    )
    return jax.shard_map(
        per_device, mesh=mesh, in_specs=placed, out_specs=P(("seq", "chan"), None), check_vma=False
    )
```

```python
import functools

import jax
import jax.numpy as jnp
from jax import lax
from jax.experimental import pallas as pl
from jax.experimental.pallas import tpu as pltpu
from jax.sharding import PartitionSpec as P

MESH = pl.DeviceIdType.MESH
LANES = 128
PIECES = 3
STEP = 16
COLS = 512
F32 = jnp.float32
BF16 = jnp.bfloat16


def kernel(
    n,
    lane_groups,
    value_hbm,
    gate_hbm,
    filter_ref,
    gate_out_ref,
    analysis_hbm,
    synthesis_hbm,
    analysis_mix_hbm,
    synthesis_mix_hbm,
    angles_hbm,
    weight_ref,
    out_ref,
    value_ref,
    gate_ref,
    analysis_ref,
    synthesis_ref,
    analysis_mix,
    synthesis_mix,
    angles,
    mix_ref,
    table_ref,
    wide,
    xsend,
    xs,
    fs,
    ysend,
    yr,
    gate_out,
    weight,
    gated,
    part,
    first,
    second_send,
    second,
    f_send,
    f_recv,
    x_send,
    x_recv,
    y_send,
    y_recv,
    local_sem,
    load_sem,
    first_send_sem,
    first_recv_sem,
    second_send_sem,
    second_recv_sem,
):
    me = lax.axis_index("seq")
    chan = lax.axis_index("chan")
    core = lax.rem(chan, 2)
    side = chan // 2
    core_peer = chan + 1 - 2 * core
    side_peer = (1 - side) * 2 + core
    tokens = value_hbm.shape[0]
    nb, blk, _ = analysis_hbm.shape
    row_groups = n // lane_groups
    rows = tokens // row_groups
    piece = rows // PIECES
    sections = n.bit_length() - 1

    loads = [
        pltpu.make_async_copy(source, target, load_sem.at[at])
        for at, (source, target) in enumerate(
            (
                (value_hbm, value_ref),
                (gate_hbm, gate_ref),
                (analysis_hbm, analysis_ref),
                (analysis_mix_hbm, analysis_mix),
                (synthesis_mix_hbm, synthesis_mix),
                (angles_hbm, angles),
                (synthesis_hbm, synthesis_ref),
            )
        )
    ]
    for load in loads:
        load.start()

    barrier = pltpu.get_barrier_semaphore()
    for s in range(1, n):
        pl.semaphore_signal(barrier, inc=1, device_id={"seq": me ^ s}, device_id_type=MESH)
    pl.semaphore_signal(barrier, inc=1, device_id={"chan": core_peer}, device_id_type=MESH)
    pl.semaphore_signal(barrier, inc=1, device_id={"chan": side_peer}, device_id_type=MESH)
    pl.semaphore_wait(barrier, n + 1)

    def chunk_lanes(index):
        return pl.ds(pl.multiple_of(lax.rem(index, lane_groups) * LANES, LANES), LANES)

    def chunk_row(index):
        return pl.multiple_of((index // lane_groups) * rows, STEP)

    my_row = chunk_row(me)

    for s in range(n - 1, 0, -1):
        there = me ^ s
        pltpu.make_async_remote_copy(
            src_ref=filter_ref.at[pl.ds(chunk_row(there), rows), chunk_lanes(there)],
            dst_ref=fs.at[s],
            send_sem=f_send,
            recv_sem=f_recv,
            device_id={"seq": there},
            device_id_type=MESH,
        ).start()
    own_filter = pltpu.make_async_copy(
        filter_ref.at[pl.ds(my_row, rows), chunk_lanes(me)], fs.at[0], local_sem.at[0]
    )
    own_filter.start()
    weight_copy = pltpu.make_async_copy(weight_ref, weight, local_sem.at[1])
    weight_copy.start()
    gate_copy = pltpu.make_async_copy(gate_out_ref, gate_out, local_sem.at[2])
    gate_copy.start()

    for load in loads:
        load.wait()

    wide[...] = jnp.zeros_like(wide)
    for which, source in enumerate((analysis_mix, synthesis_mix)):
        for k in range(nb):
            at = (which * nb + k) * nb
            wide[pl.ds(at, nb), :] = source[k].astype(F32)
    mix_ref[...] = wide[...].T

    def analyse(step, carry):
        t = lane_groups - 1 - step
        lanes = pl.ds(
            pl.multiple_of((lax.rem(me, lane_groups) ^ t) * LANES, LANES), LANES
        )
        mixed = (gate_ref[:, lanes].astype(F32) * value_ref[:, lanes].astype(F32)).astype(BF16)
        inner = [
            jnp.dot(
                analysis_ref[k], mixed[k * blk : (k + 1) * blk], preferred_element_type=F32
            )
            .astype(BF16)
            .astype(F32)
            for k in range(nb)
        ]
        for k in range(nb):
            total = mix_ref[:, k * nb : k * nb + 1] * inner[0]
            for other in range(1, nb):
                at = k * nb + other
                total += mix_ref[:, at : at + 1] * inner[other]
            xsend[t, pl.ds(k * blk, blk), :] = total.astype(BF16)
        return carry

    lax.fori_loop(0, lane_groups, analyse, 0)
    xs[0] = xsend[0, pl.ds(my_row, rows), :]
    for p in range(PIECES):
        for s in range(n - 1, 0, -1):
            there = me ^ s
            pltpu.make_async_remote_copy(
                src_ref=xsend.at[
                    s % lane_groups,
                    pl.ds(pl.multiple_of(chunk_row(there) + p * piece, STEP), piece),
                ],
                dst_ref=xs.at[s, pl.ds(p * piece, piece)],
                send_sem=x_send.at[p],
                recv_sem=x_recv.at[p],
                device_id={"seq": there},
                device_id_type=MESH,
            ).start()

    for k in range(nb):
        theta = angles[:, pl.ds(k * blk, blk)]
        cosine, sine = jnp.cos(theta), jnp.sin(theta)
        for b in range(sections):
            sign = (1 - 2 * (me >> b & 1)).astype(F32)
            wide[pl.ds(b, 1), :] = cosine[b : b + 1]
            wide[pl.ds(sections + b, 1), :] = sine[b : b + 1] * sign
        table_ref[pl.ds(k * blk, blk), :] = wide[...].T

    def others(ref, p):
        return ref.at[pl.ds(1, n - 1), pl.ds(p * piece, piece)]

    def wait_bytes(ref, sem):
        pltpu.make_async_copy(ref, ref, sem).wait()

    own_filter.wait()
    wait_bytes(fs.at[pl.ds(1, n - 1)], f_recv)
    for p in range(PIECES):
        wait_bytes(others(xs, p), x_recv.at[p])

        def rotate(step, carry):
            at = pl.multiple_of(p * piece + step * STEP, STEP)
            here = pl.multiple_of(my_row + at, STEP)
            spec = [xs[s, pl.ds(at, STEP), :].astype(F32) for s in range(n)]
            cosine = [table_ref[pl.ds(here, STEP), b : b + 1] for b in range(sections)]
            sine = [
                table_ref[pl.ds(here, STEP), sections + b : sections + b + 1]
                for b in range(sections)
            ]

            def section(spec, b, flip):
                plus, minus = (sine[b], -sine[b]) if flip > 0 else (-sine[b], sine[b])
                return [
                    cosine[b] * spec[s] + (minus if s >> b & 1 else plus) * spec[s ^ (1 << b)]
                    for s in range(n)
                ]

            for b in range(sections):
                spec = section(spec, b, 1)
            spec = [spec[s] * fs[s, pl.ds(at, STEP), :].astype(F32) for s in range(n)]
            for b in reversed(range(sections)):
                spec = section(spec, b, -1)
            yr[0, pl.ds(here, STEP), :] = spec[0].astype(BF16)
            for s in range(1, n):
                ysend[s, pl.ds(at, STEP), :] = spec[s].astype(BF16)
            return carry

        lax.fori_loop(0, piece // STEP, rotate, 0)
        for s in range(n - 1, 0, -1):
            pltpu.make_async_remote_copy(
                src_ref=ysend.at[s, pl.ds(p * piece, piece)],
                dst_ref=yr.at[
                    s % lane_groups, pl.ds(pl.multiple_of(my_row + p * piece, STEP), piece)
                ],
                send_sem=y_send.at[p],
                recv_sem=y_recv.at[s],
                device_id={"seq": me ^ s},
                device_id_type=MESH,
            ).start()

    gate_copy.wait()

    def arrive(t):
        @pl.when(t > 0)
        def _():
            wait_bytes(ysend.at[t], y_recv.at[t])

        for u in range(1, row_groups):
            wait_bytes(ysend.at[u * lane_groups + t], y_recv.at[u * lane_groups + t])

    def group(t):
        lanes = pl.ds(
            pl.multiple_of((lax.rem(me, lane_groups) ^ t) * LANES, LANES), LANES
        )
        back = [yr[t, pl.ds(k * blk, blk), :].astype(F32) for k in range(nb)]
        for k in range(nb):
            at = nb * nb + k * nb
            total = mix_ref[:, at : at + 1] * back[0]
            for other in range(1, nb):
                total += mix_ref[:, at + other : at + other + 1] * back[other]
            conv = jnp.dot(synthesis_ref[k], total.astype(BF16), preferred_element_type=F32)
            gated[pl.ds(k * blk, blk), lanes] = (
                gate_out[pl.ds(k * blk, blk), lanes].astype(F32) * conv
            ).astype(BF16)

    def synthesise(pair, carry):
        arrive(2 * pair)
        arrive(2 * pair + 1)
        group(2 * pair)
        group(2 * pair + 1)
        return carry

    lax.fori_loop(0, lane_groups // 2, synthesise, 0)
    weight_copy.wait()

    share = tokens // 4
    blocks = weight.shape[1] // COLS

    def columns(q):
        return pl.ds(pl.multiple_of(q * COLS, COLS), COLS)

    def to_core(q):
        return pltpu.make_async_remote_copy(
            src_ref=part.at[q, 1 - core],
            dst_ref=first.at[q],
            send_sem=first_send_sem.at[q],
            recv_sem=first_recv_sem.at[q],
            device_id={"chan": core_peer},
            device_id_type=MESH,
        )

    def to_side(q):
        return pltpu.make_async_remote_copy(
            src_ref=second_send.at[q],
            dst_ref=second.at[q],
            send_sem=second_send_sem.at[q],
            recv_sem=second_recv_sem.at[q],
            device_id={"chan": side_peer},
            device_id_type=MESH,
        )

    def forward(q):
        to_core(q).wait_recv()
        second_send[q] = (
            part[q, core, 1 - side].astype(F32) + first[q, 1 - side].astype(F32)
        ).astype(BF16)
        to_side(q).start()

    def project(q, carry):
        product = jnp.dot(gated[...], weight[:, columns(q)], preferred_element_type=F32)
        for g in range(4):
            part[q, g % 2, g // 2] = product[g * share : (g + 1) * share].astype(BF16)
        to_core(q).start()

        @pl.when(q > 0)
        def _():
            forward(q - 1)

        return carry

    lax.fori_loop(0, blocks, project, 0)
    forward(blocks - 1)

    def finish(q, carry):
        to_side(q).wait_recv()
        out_ref[:, columns(q)] = (
            part[q, core, side].astype(F32)
            + first[q, side].astype(F32)
            + second[q].astype(F32)
        ).astype(BF16)
        to_core(q).wait_send()
        to_side(q).wait_send()
        return carry

    lax.fori_loop(0, blocks, finish, 0)
    wait_bytes(fs.at[pl.ds(1, n - 1)], f_send)
    for p in range(PIECES):
        wait_bytes(others(xs, p), x_send.at[p])
        wait_bytes(others(ysend, p), y_send.at[p])


def per_device(
    value_in,
    gate_in,
    gate_out,
    spectral_filter,
    analysis_blocks,
    analysis_mix,
    synthesis_blocks,
    synthesis_mix,
    angles,
    out_weight,
):
    tokens, chans = value_in.shape
    analysis_mix = analysis_mix.transpose(1, 2, 0)
    synthesis_mix = synthesis_mix.transpose(1, 2, 0)
    blk = analysis_blocks.shape[1]
    width = out_weight.shape[1]
    n = lax.axis_size("seq")
    lane_groups = min(n, chans // LANES)
    rows = tokens // (n // lane_groups)
    blocks = width // COLS
    share = tokens // 4
    vmem = pl.BlockSpec(memory_space=pltpu.VMEM)
    hbm = pl.BlockSpec(memory_space=pltpu.HBM)
    chunk = pltpu.VMEM((n, rows, LANES), BF16)
    whole = pltpu.VMEM((lane_groups, tokens, LANES), BF16)
    return pl.pallas_call(
        functools.partial(kernel, n, lane_groups),
        out_shape=jax.ShapeDtypeStruct((share, width), BF16),
        in_specs=[hbm] * 10,
        out_specs=vmem,
        scratch_shapes=[
            pltpu.VMEM((tokens, chans), BF16),
            pltpu.VMEM((tokens, chans), BF16),
            pltpu.VMEM(analysis_blocks.shape, BF16),
            pltpu.VMEM(synthesis_blocks.shape, BF16),
            pltpu.VMEM(analysis_mix.shape, BF16),
            pltpu.VMEM(synthesis_mix.shape, BF16),
            pltpu.VMEM(angles.shape, F32),
            pltpu.VMEM((blk, LANES), F32),
            pltpu.VMEM((tokens, LANES), F32),
            pltpu.VMEM((LANES, blk), F32),
            whole,
            chunk,
            chunk,
            chunk,
            whole,
            pltpu.VMEM((tokens, chans), BF16),
            pltpu.VMEM(out_weight.shape, BF16),
            pltpu.VMEM((tokens, chans), BF16),
            pltpu.VMEM((blocks, 2, 2, share, COLS), BF16),
            pltpu.VMEM((blocks, 2, share, COLS), BF16),
            pltpu.VMEM((blocks, share, COLS), BF16),
            pltpu.VMEM((blocks, share, COLS), BF16),
            pltpu.SemaphoreType.DMA,
            pltpu.SemaphoreType.DMA,
            pltpu.SemaphoreType.DMA((PIECES,)),
            pltpu.SemaphoreType.DMA((PIECES,)),
            pltpu.SemaphoreType.DMA((PIECES,)),
            pltpu.SemaphoreType.DMA((n,)),
            pltpu.SemaphoreType.DMA((3,)),
            pltpu.SemaphoreType.DMA((7,)),
            pltpu.SemaphoreType.DMA((blocks,)),
            pltpu.SemaphoreType.DMA((blocks,)),
            pltpu.SemaphoreType.DMA((blocks,)),
            pltpu.SemaphoreType.DMA((blocks,)),
        ],
        compiler_params=pltpu.CompilerParams(
            collective_id=0, has_side_effects=True, vmem_limit_bytes=62 * 2**20
        ),
    )(
        value_in,
        gate_in,
        spectral_filter,
        gate_out,
        analysis_blocks,
        synthesis_blocks,
        analysis_mix,
        synthesis_mix,
        angles,
        out_weight,
    )


def solution(mesh):
    placed = (
        P("seq", "chan"),
        P("seq", "chan"),
        P("seq", "chan"),
        P("seq", "chan"),
        P(),
        P(),
        P(),
        P(),
        P(),
        P("chan", None),
    )
    return jax.shard_map(
        per_device, mesh=mesh, in_specs=placed, out_specs=P(("seq", "chan"), None), check_vma=False
    )
```
